256 devices in a mesh: gx: 8 (over x, z_lo), gy: 32 (over y, z_hi, core).
Axes of the slice: x: 4, y: 4, z: 8 (z_hi: 4, z_lo: 2; z = z_hi * 2 + z_lo), core: 2. Of those that a mesh axis runs over, the one named last changes fastest.
Arguments:
- coeff: float32 [2, 64, 8, 32, 4096], P(None, None, 'gx', 'gy'), may hold values from -6 to 6
- phase_x: float32 [4, 2, 64, 8], replicated, may hold values from -3.140625 to 3.140625
- phase_y: float32 [4, 2, 64, 32], replicated, may hold values from -3.140625 to 3.140625
- phase_q: float32 [4, 2, 64, 4096], replicated, may hold values from -3.140625 to 3.140625
- interp: float32 [4, 64, 64], replicated, may hold values from -0.07 to 0.57
Outputs:
- result: float32 [2, 64, 8, 32, 4096], P(None, None, 'gx', 'gy')
The draws below stay inside these ranges and needn't reach their ends.
All inputs are finite; a program needn't handle non-finite values.
Results may differ from the reference program's by a relative error of at most 0.00011.
Values sent between devices are 32-bit elements; how exact they have to be, the bound alone decides.
A program may use at most 128 MiB of HBM per device.

```python
import jax
import jax.numpy as jnp
from jax import lax

K = 64
LEVELS = 4
Q = 4096
GXB = 8
GYB = 32
N_GX = 8
N_GY = 32


def draw_interp(key, part):
    key = jax.random.fold_in(key, 11)
    rows = jnp.arange(K)[:, None]
    cols = jnp.arange(K)[None, :]
    eye_mask = jnp.where(rows == cols, 1.0, 0.0).astype(jnp.float32)
    limit = 0.065
    noise = jax.random.uniform(key, (4, K, K), jnp.float32, -limit, limit)
    return (0.5 * eye_mask[None] + noise).astype(jnp.float32)


def steps_of(rng, shape, shards, least, high):
    def one(position, parts):
        steps = jax.random.uniform(jax.random.fold_in(jax.random.fold_in(rng, 6), position), (parts,), jnp.float32, least / len(shards), high / len(shards))
        return jnp.repeat(jnp.exp(steps), shape[position] // parts).reshape((-1,) + (1,) * (len(shape) - position - 1))

    level = one(*shards[0])
    for cut in shards[1:]:
        level = level * one(*cut)
    return level


def bell_draw(rng, dims, width, bound, pieces=(), held_as=jnp.bfloat16):
    values = jax.random.normal(rng, dims, jnp.float32) * width
    if len(pieces) > 0:
        values = steps_of(rng, dims, pieces, -0.22, 0.18) * values
    return jnp.clip(values, min=-bound, max=bound).astype(held_as)


def setup_inputs(seed: int = 0) -> dict:
    arg_keys = jax.random.split(jax.random.key(seed), 6)
    return {
        "coeff": bell_draw(arg_keys[0], (2, K, GXB, GYB, Q), 1.0, 6.0, ((2, 8), (3, 32)), jnp.float32),
        "phase_x": jnp.clip(jax.random.uniform(arg_keys[1], (LEVELS, 2, K, GXB), jnp.float32, -3.140625, 3.140625), -3.140625, 3.140625),
        "phase_y": jnp.clip(jax.random.uniform(arg_keys[2], (LEVELS, 2, K, GYB), jnp.float32, -3.140625, 3.140625), -3.140625, 3.140625),
        "phase_q": jnp.clip(jax.random.uniform(arg_keys[3], (LEVELS, 2, K, Q), jnp.float32, -3.140625, 3.140625), -3.140625, 3.140625),
        "interp": draw_interp(jax.random.fold_in(arg_keys[5], 71), 0),
    }


def flip_bit(values, axis_no, bit_no):
    length = values.shape[axis_no]
    new_shape = values.shape[:axis_no] + (length >> (bit_no + 1), 2, 1 << bit_no) + values.shape[axis_no + 1:]
    return jnp.flip(values.reshape(new_shape), axis_no + 1).reshape(values.shape)


def apply_blocks(values, interp, bit_x, bit_y):
    grouped = values.reshape(values.shape[0], values.shape[1], values.shape[2] >> (bit_x + 1), 2, 1 << bit_x,
                             values.shape[3] >> (bit_y + 1), 2, 1 << bit_y, values.shape[4])
    blocks = interp.reshape(2, 2, interp.shape[1], interp.shape[2])
    mapped = jnp.einsum("xytk,rkaxbcyeq->rtaxbcyeq", blocks, grouped, precision=lax.Precision.HIGHEST)
    return mapped.reshape(values.shape)


def rotate_in(values, angle):
    cosine = jnp.cos(angle)
    sine_part = jnp.sin(angle)
    return jnp.stack([values[0] * cosine + values[1] * sine_part, values[1] * cosine - values[0] * sine_part])


def rotate_out(values, angle):
    cosine = jnp.cos(angle)
    sine_part = jnp.sin(angle)
    return jnp.stack([values[0] * cosine - values[1] * sine_part, values[0] * sine_part + values[1] * cosine])


def full_angles(part_x, part_y, part_q):
    return (part_x[:, :, None, None] + part_y[:, None, :, None]) + part_q[:, None, None, :]


def level_full(coeffs, interp, angle_in, angle_out, bit_x, bit_y):
    turned = rotate_in(coeffs, angle_in)
    summed = turned + flip_bit(turned, 2, bit_x)
    summed = summed + flip_bit(summed, 3, bit_y)
    return rotate_out(apply_blocks(summed, interp, bit_x, bit_y), angle_out)


def reference(coeff, phase_x, phase_y, phase_q, interp):
    bits_x = N_GX.bit_length() - 1
    bits_y = N_GY.bit_length() - 1
    coeffs = coeff
    for step_no in range(LEVELS):
        bit_x = (bits_x - 1 - step_no) % bits_x
        bit_y = (bits_y - 1 - step_no) % bits_y
        angle_in = full_angles(phase_x[step_no, 0], phase_y[step_no, 0], phase_q[step_no, 0])
        angle_out = full_angles(phase_x[step_no, 1], phase_y[step_no, 1], phase_q[step_no, 1])
        coeffs = level_full(coeffs, interp, angle_in, angle_out, bit_x, bit_y)
    return coeffs
```

```python
import jax
import jax.numpy as jnp
from jax import lax
from jax.experimental import pallas as pl
from jax.experimental.pallas import tpu as pltpu
from jax.sharding import PartitionSpec as P

MESH = pl.DeviceIdType.MESH
F32 = jnp.float32
BF16 = jnp.bfloat16
K = 64
LANES = 128


def flip(bit, other):
    return bit + other - 2 * bit * other


def flip_bits(value, mask, bits):
    total = 0
    for n in range(bits):
        total = total + (1 << n) * flip(value // (1 << n) % 2, mask // (1 << n) % 2)
    return total


def lane_bit(shape, width):
    return lax.broadcasted_iota(jnp.int32, shape, len(shape) - 1) // width % 2 == 0


def lane_transpose(parts):
    low64 = lane_bit(parts[0].shape, 64)
    low32 = lane_bit(parts[0].shape, 32)
    a, b, c, d = parts
    a, c = jnp.where(low64, a, pltpu.roll(c, 64, 1)), jnp.where(low64, pltpu.roll(a, 64, 1), c)
    b, d = jnp.where(low64, b, pltpu.roll(d, 64, 1)), jnp.where(low64, pltpu.roll(b, 64, 1), d)
    a, b = jnp.where(low32, a, pltpu.roll(b, 32, 1)), jnp.where(low32, pltpu.roll(a, 96, 1), b)
    c, d = jnp.where(low32, c, pltpu.roll(d, 32, 1)), jnp.where(low32, pltpu.roll(c, 96, 1), d)
    return a, b, c, d


def pack(re, im):
    return lane_transpose((re[:32], re[32:], im[:32], im[32:]))


def unpack(parts):
    a, b, c, d = lane_transpose(parts)
    return jnp.concatenate([a, b], 0), jnp.concatenate([c, d], 0)


def turn(re, im, cos, sin):
    return re * cos - im * sin, re * sin + im * cos


def split_rows(re, im):
    both = jnp.concatenate([re, im], 1)
    high = both.astype(BF16)
    low = (both - high.astype(F32)).astype(BF16)
    return jnp.concatenate([high, low, high], 0)


def split_columns(blocks):
    high = blocks.astype(BF16).astype(F32)
    low = blocks - high
    return jnp.concatenate([high, high, low], 1).astype(BF16)


def kernel(
    coeff, phase_x, phase_y, phase_q, interp, out,
    field, first, second, send_a, recv_a, send_b, recv_b, recv_z, recv_x,
    state, factor, x_cos, x_sin, y_cos, y_sin, q_own, q_cos, q_sin, last, q_last, staged,
    maps, own_map,
    field_sem, q_sem, first_send, first_recv, second_send, second_recv,
    a_send, a_recv, b_send, b_recv, z_send, z_recv, x_send, x_recv, out_sem,
):
    gx, gy = lax.axis_index("gx"), lax.axis_index("gy")
    x2, x1, x0 = gx // 4, gx // 2 % 2, gx % 2
    y4, y3, y2, y1, core = gy // 16, gy // 8 % 2, gy // 4 % 2, gy // 2 % 2, gy % 2
    z = 4 * y2 + 2 * y1 + x0
    group = 2 * x1 + y3

    def device(fx2=0, fx1=0, fx0=0, fy4=0, fy3=0, fy2=0, fy1=0):
        return (
            4 * flip(x2, fx2) + 2 * flip(x1, fx1) + flip(x0, fx0),
            16 * flip(y4, fy4) + 8 * flip(y3, fy3) + 4 * flip(y2, fy2) + 2 * flip(y1, fy1) + core,
        )

    def spread_device(slot):
        return device(
            fy2=slot // 16, fy1=slot // 8 % 2, fx0=slot // 4 % 2, fx1=slot // 2 % 2, fy3=slot % 2
        )

    def gather_device(slot):
        return device(
            fy4=slot // 16, fx0=slot // 8 % 2, fy2=slot // 4 % 2, fx1=slot // 2 % 2, fy3=slot % 2
        )

    barrier = pltpu.get_barrier_semaphore()

    def load(i):
        for fx in range(2):
            for fy in range(2):
                block = 16 * flip(x2, fx) + 8 * flip(y4, fy) + flip_bits(z, i, 3)
                yield pltpu.make_async_copy(
                    coeff.at[:, :, block, :], field.at[i, fx, fy], field_sem.at[i, fx, fy]
                )

    for i in range(8):
        for copy in load(i):
            copy.start()
    own_block = 16 * x2 + 8 * y4 + z
    own_copy = pltpu.make_async_copy(
        phase_q.at[:, :, :, pl.ds(pl.multiple_of(own_block * LANES, LANES), LANES)], q_own, q_sem.at[0]
    )
    own_copy.start()
    last_copy = pltpu.make_async_copy(phase_q.at[3, 1], q_last, q_sem.at[1])
    last_copy.start()

    @pl.loop(1, 32)
    def _(slot):
        pl.semaphore_signal(barrier, inc=1, device_id=spread_device(slot), device_id_type=MESH)

    @pl.loop(16, 32)
    def _(slot):
        pl.semaphore_signal(barrier, inc=1, device_id=gather_device(slot), device_id_type=MESH)

    pl.semaphore_signal(barrier, inc=1, device_id=device(fx2=1), device_id_type=MESH)

    def columns(row):
        wide = jnp.broadcast_to(jnp.concatenate([row, row], 1), (LANES, LANES))
        return wide.T[:K]

    angle = phase_x[0, 0, pl.ds(gx, 1), :] + phase_y[0, 0, pl.ds(gy, 1), :]
    in_cos, in_sin = columns(jnp.cos(angle)), columns(-jnp.sin(angle))
    out_angle = columns(phase_x[3, 1, pl.ds(gx, 1), :] + phase_y[3, 1, pl.ds(gy, 1), :])

    def rotate(i, fx, fy):
        re, im = turn(field[i, fx, fy, 0], field[i, fx, fy, 1], in_cos, in_sin)
        field[i, fx, fy, 0] = re
        field[i, fx, fy, 1] = im

    pl.semaphore_wait(barrier, 48)

    x_first = [i % 2 == 0 for i in range(8)]
    partner_x, partner_y, partner_z = device(fx2=1), device(fy4=1), device(fy1=1)

    def first_copy(i):
        return pltpu.make_async_remote_copy(
            field.at[i, 1] if x_first[i] else field.at[i, :, 1],
            first.at[i], first_send.at[i], first_recv.at[i],
            device_id=partner_x if x_first[i] else partner_y, device_id_type=MESH,
        )

    def second_copy(i):
        return pltpu.make_async_remote_copy(
            field.at[i, 0, 1] if x_first[i] else field.at[i, 1, 0],
            second.at[i], second_send.at[i], second_recv.at[i],
            device_id=partner_y if x_first[i] else partner_x, device_id_type=MESH,
        )

    order = [7, 6, 5, 4, 3, 2, 1, 0]
    for i in order:
        copies = list(load(i))
        for copy in copies:
            copy.wait()
        for fx, fy in ((1, 1), (1, 0) if x_first[i] else (0, 1)):
            rotate(i, fx, fy)
        first_copy(i).start()
    for i in order:
        for fx, fy in ((0, 0), (0, 1) if x_first[i] else (1, 0)):
            rotate(i, fx, fy)

    for l in range(3):
        difference = phase_x[l, 1] - phase_x[l + 1, 0]
        x_cos[l] = jnp.cos(difference)
        x_sin[l] = jnp.sin(difference)
        difference = phase_y[l, 1] - phase_y[l + 1, 0]
        y_cos[l] = jnp.cos(difference)
        y_sin[l] = jnp.sin(difference)

    @pl.loop(0, 32)
    def _(n):
        for l in range(3):
            rows = []
            for high in range(2):
                if l < 2:
                    a = n // 8 * 2 + high
                else:
                    a = n // 16 * 4 + high * 2 + n // 8 % 2
                for low in range(2):
                    b = n % 8 * 4 + low * 2 + core
                    xc, xs = x_cos[l, pl.ds(a, 1), :], x_sin[l, pl.ds(a, 1), :]
                    yc, ys = y_cos[l, pl.ds(b, 1), :], y_sin[l, pl.ds(b, 1), :]
                    row = jnp.concatenate(turn(xc, xs, yc, ys), 1)
                    rows.append(jnp.broadcast_to(row, (32, LANES)))
            factor[l, n] = jnp.concatenate(rows, 0).T

    own_copy.wait()
    for l in range(4):
        value = -q_own[0, 0] if l == 0 else q_own[l - 1, 1] - q_own[l, 0]
        value = pltpu.roll(value, (128 - 32 * group) % 128, 1)
        value = jnp.where(lax.broadcasted_iota(jnp.int32, value.shape, 1) < 32, value, 0.0)
        value = value + pltpu.roll(value, 32, 1)
        value = value + pltpu.roll(value, 64, 1)
        q_cos[l] = jnp.cos(value)
        q_sin[l] = jnp.sin(value)
    maps[...] = jnp.concatenate([split_columns(interp[c]) for c in range(4)], 0)
    own_map[...] = split_columns(interp[2 * x2 + y1])

    for i in order:
        first_copy(i).wait()
        fx, fy = (0, 1) if x_first[i] else (1, 0)
        field[i, fx, fy] = field[i, fx, fy] + first[i, 1]
        second_copy(i).start()
        field[i, 0, 0] = field[i, 0, 0] + first[i, 0]

    def spread_copy(slot):
        return pltpu.make_async_remote_copy(
            send_a.at[slot], recv_a.at[slot], a_send, a_recv,
            device_id=spread_device(slot), device_id_type=MESH,
        )

    for i in order:
        second_copy(i).wait()
        parts = pack(field[i, 0, 0, 0] + second[i, 0], field[i, 0, 0, 1] + second[i, 1])
        for g in range(4):
            send_a[4 * i + flip_bits(group, g, 2)] = parts[g]
        for g in range(4):
            if i == 0 and g == 0:
                recv_a[0] = send_a[0]
            else:
                spread_copy(4 * i + g).start()

    last_copy.wait()

    @pl.loop(0, 32)
    def _(block):
        value = out_angle + q_last[:, pl.ds(pl.multiple_of(block * LANES, LANES), LANES)]
        last[block, 0] = jnp.cos(value)
        last[block, 1] = jnp.sin(value)

    pltpu.make_async_remote_copy(
        send_a.at[pl.ds(1, 31)], recv_a.at[pl.ds(1, 31)], a_send, a_recv,
        device_id=partner_x, device_id_type=MESH,
    ).wait()

    def mapped(re, im):
        return jnp.dot(maps[...], split_rows(re, im), preferred_element_type=F32)

    def add_turned(total, values, l, place):
        for c in range(4):
            cos, sin = factor[l, place(c), :K], factor[l, place(c), K:]
            re, im = turn(values[c * K:(c + 1) * K, :LANES], values[c * K:(c + 1) * K, LANES:], cos, sin)
            total[c] = (re, im) if total[c] is None else (total[c][0] + re, total[c][1] + im)

    def finish(re, im, l):
        return turn(re, im, q_cos[l], q_sin[l])

    @pl.loop(0, 2)
    def _(c2):
        total = [None] * 4
        for s1 in range(2):
            for s3 in range(2):
                messages = []
                for s0 in range(2):
                    for t1 in range(2):
                        place = 4 * flip(y2, c2) + 2 * flip(y1, t1) + flip(x0, s0)
                        messages.append(recv_a[4 * place + 2 * flip(x1, s1) + flip(y3, s3)])
                re, im = finish(*unpack(messages), 0)
                add_turned(
                    total, mapped(re, im), 0,
                    lambda c: (c // 2 * 2 + s1) * 8 + c % 2 * 4 + s3 * 2 + c2,
                )
        for c in range(4):
            re, im = finish(*total[c], 1)
            state[0, 2 * c + c2, 0] = re
            state[0, 2 * c + c2, 1] = im

    @pl.loop(0, 4)
    def _(c):
        total = [None] * 4
        for s2 in range(2):
            add_turned(
                total, mapped(state[0, 2 * c + s2, 0], state[0, 2 * c + s2, 1]), 1,
                lambda d: (c // 2 * 2 + d // 2) * 8 + c % 2 * 4 + d % 2 * 2 + s2,
            )
        low = lane_bit((K, LANES), 64)
        for d3 in range(2):
            re, im = finish(*(
                jnp.where(low, a + pltpu.roll(a, 64, 1), b + pltpu.roll(b, 64, 1))
                for a, b in zip(total[d3], total[2 + d3])
            ), 2)
            state[1, 2 * c + d3, 0] = re
            state[1, 2 * c + d3, 1] = im

    def gather_copy(slot):
        return pltpu.make_async_remote_copy(
            send_b.at[slot], recv_b.at[slot // 4, slot % 4], b_send, b_recv.at[slot // 4],
            device_id=gather_device(slot), device_id_type=MESH,
        )

    for r4 in range(2):
        for r3 in range(2):
            d4, d3 = flip(y4, r4), flip(y3, r3)
            total = [None] * 4
            for s in range(2):
                n = 4 * s + 2 * d4 + d3
                add_turned(
                    total, mapped(state[1, n, 0], state[1, n, 1]), 2,
                    lambda c: (s * 2 + c // 2) * 8 + 4 * d4 + 2 * d3 + c % 2,
                )
            low = lane_bit((K, LANES), 32)
            for c2 in range(2):
                re, im = finish(*(
                    jnp.where(low, a + pltpu.roll(a, 96, 1), b + pltpu.roll(b, 32, 1))
                    for a, b in zip(total[c2], total[2 + c2])
                ), 3)
                parts = pack(re, im)
                for e1 in range(2):
                    for e0 in range(2):
                        slot = 16 * r4 + 8 * flip(x0, e0) + 4 * flip(y2, c2) + 2 * flip(x1, e1) + r3
                        send_b[slot] = parts[2 * e1 + e0]
            for slot in range(32):
                if slot // 16 == r4 and slot % 2 == r3:
                    if slot == 0:
                        recv_b[0, 0] = send_b[0]
                    else:
                        gather_copy(slot).start()

    def z_copy(i):
        return pltpu.make_async_remote_copy(
            recv_b.at[i], recv_z.at[i], z_send.at[i], z_recv.at[i],
            device_id=partner_z, device_id_type=MESH,
        )

    def x_copy(i):
        return pltpu.make_async_remote_copy(
            recv_b.at[i] if i < 8 else recv_z.at[i - 8], recv_x.at[i], x_send.at[i], x_recv.at[i],
            device_id=partner_x, device_id_type=MESH,
        )

    def result_copy(block):
        return pltpu.make_async_copy(staged.at[block], out.at[:, :, block, :], out_sem.at[block])

    def expand(source, i, fx, fz):
        block = (
            16 * flip(x2, fx) + 8 * flip(y4, i // 4) + 4 * flip(y2, i % 2) + 2 * flip(y1, fz)
            + flip(x0, i // 2 % 2)
        )
        re, im = unpack([source[flip_bits(group, g, 2)] for g in range(4)])
        values = jnp.dot(own_map[...], split_rows(re, im), preferred_element_type=F32)
        re, im = turn(values[:, :LANES], values[:, LANES:], last[block, 0], last[block, 1])
        staged[block, 0] = re
        staged[block, 1] = im
        result_copy(block).start()

    for i in range(8):
        arrived = recv_b.at[0, pl.ds(1, 3)] if i == 0 else recv_b.at[i]
        pltpu.make_async_remote_copy(
            arrived, arrived, b_send, b_recv.at[i], device_id=partner_x, device_id_type=MESH
        ).wait_recv()
        z_copy(i).start()
        x_copy(i).start()
    for i in range(8):
        expand(recv_b.at[i], i, 0, 0)
    for i in range(8):
        z_copy(i).wait_recv()
        x_copy(8 + i).start()
        expand(recv_z.at[i], i, 0, 1)
    for i in range(16):
        x_copy(i).wait_recv()
        expand(recv_x.at[i], i % 8, 1, i // 8)
    for i in range(8):
        z_copy(i).wait_send()
    for i in range(16):
        x_copy(i).wait_send()
    pltpu.make_async_remote_copy(
        send_b.at[pl.ds(1, 31)], send_b.at[pl.ds(1, 31)], b_send, b_recv.at[0],
        device_id=partner_x, device_id_type=MESH,
    ).wait_send()
    for block in range(32):
        result_copy(block).wait()


def per_device(coeff, phase_x, phase_y, phase_q, interp):
    field = (2, K, LANES)
    message = (32, LANES)
    dma = pltpu.SemaphoreType.DMA
    result = pl.pallas_call(
        kernel,
        out_shape=jax.ShapeDtypeStruct((2, K, 32, LANES), F32),
        in_specs=[
            pl.BlockSpec(memory_space=pl.ANY),
            pl.BlockSpec(memory_space=pltpu.VMEM),
            pl.BlockSpec(memory_space=pltpu.VMEM),
            pl.BlockSpec(memory_space=pl.ANY),
            pl.BlockSpec(memory_space=pltpu.VMEM),
        ],
        out_specs=pl.BlockSpec(memory_space=pl.ANY),
        scratch_shapes=[
            pltpu.VMEM((8, 2, 2, *field), F32),
            pltpu.VMEM((8, 2, *field), F32),
            pltpu.VMEM((8, *field), F32),
            pltpu.VMEM((32, *message), F32),
            pltpu.VMEM((32, *message), F32),
            pltpu.VMEM((32, *message), F32),
            pltpu.VMEM((8, 4, *message), F32),
            pltpu.VMEM((8, 4, *message), F32),
            pltpu.VMEM((16, 4, *message), F32),
            pltpu.VMEM((2, 8, *field), F32),
            pltpu.VMEM((3, 32, LANES, LANES), F32),
            pltpu.VMEM((3, 8, K), F32),
            pltpu.VMEM((3, 8, K), F32),
            pltpu.VMEM((3, 32, K), F32),
            pltpu.VMEM((3, 32, K), F32),
            pltpu.VMEM((4, 2, K, LANES), F32),
            pltpu.VMEM((4, K, LANES), F32),
            pltpu.VMEM((4, K, LANES), F32),
            pltpu.VMEM((32, *field), F32),
            pltpu.VMEM((K, 32 * LANES), F32),
            pltpu.VMEM((32, *field), F32),
            pltpu.VMEM((4 * K, 3 * K), BF16),
            pltpu.VMEM((K, 3 * K), BF16),
            dma((8, 2, 2)), dma((2,)), dma((8,)), dma((8,)), dma((8,)), dma((8,)),
            dma, dma, dma, dma((8,)), dma((8,)), dma((8,)), dma((16,)), dma((16,)), dma((32,)),
        ],
        compiler_params=pltpu.CompilerParams(
            collective_id=0, has_side_effects=True, vmem_limit_bytes=48 * 1024 * 1024
        ),
    )(
        coeff.reshape(2, K, 32, LANES),
        phase_x.transpose(0, 1, 3, 2),
        phase_y.transpose(0, 1, 3, 2),
        phase_q,
        interp,
    )
    return result.reshape(2, K, 1, 1, 32 * LANES)


def solution(mesh):
    placed = (P(None, None, "gx", "gy", None), P(), P(), P(), P())
    return jax.shard_map(
        per_device,
        mesh=mesh,
        in_specs=placed,
        out_specs=P(None, None, "gx", "gy", None),
        check_vma=False,
    )
```

```python
import jax
import jax.numpy as jnp
import numpy as np
from jax import lax
from jax.experimental import pallas as pl
from jax.experimental.pallas import tpu as pltpu
from jax.sharding import PartitionSpec as P

MESH = pl.DeviceIdType.MESH
F32 = jnp.float32
BF16 = jnp.bfloat16
K = 64
LANES = 128
ORDER = (4, 5, 6, 2, 3, 7, 1, 0)
AHEAD = 4
LAG = 3
BEHIND = 3
GATHER_ORDER = (0, 4, 2, 6, 3, 7, 1, 5)


def flip(bit, other):
    return bit + other - 2 * bit * other


def flip_bits(value, mask, bits):
    total = 0
    for n in range(bits):
        total = total + (1 << n) * flip(value // (1 << n) % 2, mask // (1 << n) % 2)
    return total


def lane_bit(shape, width):
    return lax.broadcasted_iota(jnp.int32, shape, len(shape) - 1) // width % 2 == 0


def lane_transpose(parts):
    low64 = lane_bit(parts[0].shape, 64)
    low32 = lane_bit(parts[0].shape, 32)
    a, b, c, d = parts
    a, c = jnp.where(low64, a, pltpu.roll(c, 64, 1)), jnp.where(low64, pltpu.roll(a, 64, 1), c)
    b, d = jnp.where(low64, b, pltpu.roll(d, 64, 1)), jnp.where(low64, pltpu.roll(b, 64, 1), d)
    a, b = jnp.where(low32, a, pltpu.roll(b, 32, 1)), jnp.where(low32, pltpu.roll(a, 96, 1), b)
    c, d = jnp.where(low32, c, pltpu.roll(d, 32, 1)), jnp.where(low32, pltpu.roll(c, 96, 1), d)
    return a, b, c, d


def pack(re, im):
    return lane_transpose((re[:32], re[32:], im[:32], im[32:]))


def unpack(parts):
    a, b, c, d = lane_transpose(parts)
    return jnp.concatenate([a, b], 0), jnp.concatenate([c, d], 0)


def cos_sin(angle):
    turns = jnp.round(angle * (2 / np.pi))
    rest = angle - turns * 1.5703125
    rest = rest - turns * 4.837512969970703125e-4
    rest = rest - turns * 7.54978995489188216e-8
    square = rest * rest
    sine = rest + rest * square * (
        -1.6666654611e-1 + square * (8.3321608736e-3 + square * -1.9515295891e-4)
    )
    cosine = 1.0 - 0.5 * square + square * square * (
        4.166664568298827e-2 + square * (-1.388731625493765e-3 + square * 2.443315711809948e-5)
    )
    quarter = turns.astype(jnp.int32) & 3
    odd = (quarter & 1) == 1
    cos, sin = jnp.where(odd, sine, cosine), jnp.where(odd, cosine, sine)
    cos = jnp.where((quarter == 1) | (quarter == 2), -cos, cos)
    return cos, jnp.where(quarter >= 2, -sin, sin)


def turn(re, im, cos, sin):
    return re * cos - im * sin, re * sin + im * cos


def split_rows(re, im):
    both = jnp.concatenate([re, im], 1)
    high = both.astype(BF16)
    low = (both - high.astype(F32)).astype(BF16)
    return jnp.concatenate([high, low, high], 0)


def split_columns(blocks):
    high = blocks.astype(BF16).astype(F32)
    low = blocks - high
    return jnp.concatenate([high, high, low], 1).astype(BF16)


def kernel(
    coeff, x_hbm, y_hbm, phase_q, interp_hbm, out,
    phase_x, phase_y, interp, field, first, second, send_a, recv_a, send_b, recv_b, recv_z, recv_x,
    state, factor_x, factor_y, factor, x_cos, x_sin, y_cos, y_sin, q_own, q_cos, q_sin, last, q_last, staged,
    maps, own_map,
    small_sem, field_sem, q_sem, first_send, first_recv, second_send, second_recv,
    a_send, a_recv, b_send, b_recv, z_send, z_recv, x_send, x_recv, out_sem,
):
    gx, gy = lax.axis_index("gx"), lax.axis_index("gy")
    x2, x1, x0 = gx // 4, gx // 2 % 2, gx % 2
    y4, y3, y2, y1, core = gy // 16, gy // 8 % 2, gy // 4 % 2, gy // 2 % 2, gy % 2
    z = 4 * y2 + 2 * y1 + x0
    group = 2 * x1 + y3

    def device(fx2=0, fx1=0, fx0=0, fy4=0, fy3=0, fy2=0, fy1=0):
        return (
            4 * flip(x2, fx2) + 2 * flip(x1, fx1) + flip(x0, fx0),
            16 * flip(y4, fy4) + 8 * flip(y3, fy3) + 4 * flip(y2, fy2) + 2 * flip(y1, fy1) + core,
        )

    def spread_device(slot):
        return device(
            fy2=slot // 16, fy1=slot // 8 % 2, fx0=slot // 4 % 2, fx1=slot // 2 % 2, fy3=slot % 2
        )

    def gather_device(slot):
        return device(
            fy4=slot // 16, fx0=slot // 8 % 2, fy2=slot // 4 % 2, fy1=slot // 4 % 2,
            fx1=slot // 2 % 2, fy3=slot % 2,
        )

    barrier = pltpu.get_barrier_semaphore()

    def load(i):
        for fx in range(2):
            for fy in range(2):
                block = 16 * flip(x2, fx) + 8 * flip(y4, fy) + flip_bits(z, i, 3)
                yield pltpu.make_async_copy(
                    coeff.at[:, :, block, :], field.at[i, fx, fy], field_sem.at[i]
                )

    small_copies = [
        pltpu.make_async_copy(source, target, small_sem.at[n])
        for n, (source, target) in enumerate(
            ((x_hbm, phase_x), (y_hbm, phase_y), (interp_hbm, interp))
        )
    ]
    for copy in small_copies:
        copy.start()
    for i in ORDER:
        for copy in load(i):
            copy.start()
    for slot in range(1, 32):
        pl.semaphore_signal(barrier, inc=1, device_id=spread_device(slot), device_id_type=MESH)
    for slot in range(16, 32):
        pl.semaphore_signal(barrier, inc=1, device_id=gather_device(slot), device_id_type=MESH)
    pl.semaphore_signal(barrier, inc=1, device_id=device(fx2=1), device_id_type=MESH)
    own_block = 16 * x2 + 8 * y4 + z
    own_copy = pltpu.make_async_copy(
        phase_q.at[:, :, :, pl.ds(pl.multiple_of(own_block * LANES, LANES), LANES)], q_own, q_sem.at[0]
    )
    own_copy.start()
    last_copy = pltpu.make_async_copy(phase_q.at[3, 1], q_last, q_sem.at[1])
    last_copy.start()

    def columns(row):
        wide = jnp.broadcast_to(jnp.concatenate([row, row], 1), (LANES, LANES))
        return wide.T[:K]

    for copy in small_copies:
        copy.wait()
    angle = phase_x[0, 0, pl.ds(gx, 1), :] + phase_y[0, 0, pl.ds(gy, 1), :]
    in_cos, in_sin = (columns(part) for part in cos_sin(-angle))
    out_angle = columns(phase_x[3, 1, pl.ds(gx, 1), :] + phase_y[3, 1, pl.ds(gy, 1), :])

    def rotate(i, fx, fy):
        re, im = turn(field[i, fx, fy, 0], field[i, fx, fy, 1], in_cos, in_sin)
        field[i, fx, fy, 0] = re
        field[i, fx, fy, 1] = im

    pl.semaphore_wait(barrier, 48)

    x_first = [ORDER.index(i) % 2 == 0 for i in range(8)]
    partner_x, partner_y, partner_z = device(fx2=1), device(fy4=1), device(fy1=1)

    def first_copy(i):
        return pltpu.make_async_remote_copy(
            field.at[i, 1] if x_first[i] else field.at[i, :, 1],
            first.at[i], first_send, first_recv.at[i],
            device_id=partner_x if x_first[i] else partner_y, device_id_type=MESH,
        )

    def second_copy(i):
        return pltpu.make_async_remote_copy(
            field.at[i, 0, 1] if x_first[i] else field.at[i, 1, 0],
            second.at[i], second_send, second_recv.at[i],
            device_id=partner_y if x_first[i] else partner_x, device_id_type=MESH,
        )

    def part_factors():
        for l in range(3):
            difference = phase_x[l, 1] - phase_x[l + 1, 0]
            x_cos[l], x_sin[l] = cos_sin(difference)
            difference = phase_y[l, 1] - phase_y[l + 1, 0]
            y_cos[l], y_sin[l] = cos_sin(difference)

    def edge_factors(l):
        def rows(cos, sin, places, count):
            return [
                jnp.broadcast_to(
                    jnp.concatenate([cos[l, pl.ds(p, 1), :], sin[l, pl.ds(p, 1), :]], 1), (count, LANES)
                )
                for p in places
            ]

        @pl.loop(0, 4, unroll=True)
        def _(n):
            places = [2 * n + h if l < 2 else n // 2 * 4 + h * 2 + n % 2 for h in range(2)]
            factor_x[l, n] = jnp.concatenate(rows(x_cos, x_sin, places, 64), 0).T

        @pl.loop(0, 8, unroll=True)
        def _(n):
            places = [4 * n + 2 * h + core for h in range(2)] * 2
            factor_y[l, n] = jnp.concatenate(rows(y_cos, y_sin, places, 32), 0).T

    def level_factors(l):
        @pl.loop(0, 32, unroll=4)
        def _(n):
            x, y = n // 8, n % 8
            cos, sin = turn(
                factor_x[l, x, :K], factor_x[l, x, K:], factor_y[l, y, :K], factor_y[l, y, K:]
            )
            factor[l, n, :K] = cos
            factor[l, n, K:] = sin

    def small_factors():
        own_copy.wait()
        for l in range(4):
            value = -q_own[0, 0] if l == 0 else q_own[l - 1, 1] - q_own[l, 0]
            value = pltpu.roll(value, (128 - 32 * group) % 128, 1)
            value = jnp.where(lax.broadcasted_iota(jnp.int32, value.shape, 1) < 32, value, 0.0)
            value = value + pltpu.roll(value, 32, 1)
            value = value + pltpu.roll(value, 64, 1)
            q_cos[l], q_sin[l] = cos_sin(value)
        maps[...] = jnp.concatenate([split_columns(interp[c]) for c in range(4)], 0)
        own_map[...] = split_columns(interp[2 * x2 + y1])

    def last_factors():
        @pl.loop(0, 32, unroll=4)
        def _(block):
            value = out_angle + q_last[:, pl.ds(pl.multiple_of(block * LANES, LANES), LANES)]
            last[block, 0], last[block, 1] = cos_sin(value)

    def start_first(i):
        pltpu.make_async_copy(field.at[i], field.at[i], field_sem.at[i]).wait()
        for fx, fy in ((1, 1), (1, 0) if x_first[i] else (0, 1)):
            rotate(i, fx, fy)
        first_copy(i).start()
        for fx, fy in ((0, 0), (0, 1) if x_first[i] else (1, 0)):
            rotate(i, fx, fy)

    def spread_copy(slot):
        return pltpu.make_async_remote_copy(
            send_a.at[slot], recv_a.at[slot], a_send, a_recv,
            device_id=spread_device(slot), device_id_type=MESH,
        )

    def start_second(i):
        first_copy(i).wait_recv()
        fx, fy = (0, 1) if x_first[i] else (1, 0)
        field[i, fx, fy] = field[i, fx, fy] + first[i, 1]
        second_copy(i).start()
        field[i, 0, 0] = field[i, 0, 0] + first[i, 0]

    def spread(i):
        second_copy(i).wait_recv()
        parts = pack(field[i, 0, 0, 0] + second[i, 0], field[i, 0, 0, 1] + second[i, 1])
        for g in range(4):
            send_a[4 * i + flip_bits(group, g, 2)] = parts[g]
        for g in range(4):
            if i == 0 and g == 0:
                recv_a[0] = send_a[0]
            else:
                spread_copy(4 * i + g).start()

    for i in ORDER[:AHEAD]:
        start_first(i)
    part_factors()
    edge_factors(0)
    edge_factors(1)
    for n in range(8 + LAG):
        if n < 8:
            start_second(ORDER[n])
        if n + AHEAD < 8:
            start_first(ORDER[n + AHEAD])
        if n >= LAG:
            spread(ORDER[n - LAG])
        if n == 0:
            edge_factors(2)
        elif n < 4:
            level_factors(n - 1)
        elif n == 4:
            small_factors()
    last_copy.wait()
    last_factors()

    pltpu.make_async_remote_copy(
        send_a.at[pl.ds(1, 31)], recv_a.at[pl.ds(1, 31)], a_send, a_recv,
        device_id=partner_x, device_id_type=MESH,
    ).wait_recv()

    def mapped(re, im):
        return jnp.dot(maps[...], split_rows(re, im), preferred_element_type=F32)

    def add_turned(total, values, l, place):
        for c in range(4):
            cos, sin = factor[l, place(c), :K], factor[l, place(c), K:]
            re, im = turn(values[c * K:(c + 1) * K, :LANES], values[c * K:(c + 1) * K, LANES:], cos, sin)
            total[c] = (re, im) if total[c] is None else (total[c][0] + re, total[c][1] + im)

    def finish(re, im, l):
        return turn(re, im, q_cos[l], q_sin[l])

    @pl.loop(0, 2, unroll=True)
    def _(c2):
        total = [None] * 4
        for s1 in range(2):
            for s3 in range(2):
                messages = []
                for s0 in range(2):
                    for t1 in range(2):
                        place = 4 * flip(y2, c2) + 2 * flip(y1, t1) + flip(x0, s0)
                        messages.append(recv_a[4 * place + 2 * flip(x1, s1) + flip(y3, s3)])
                re, im = finish(*unpack(messages), 0)
                add_turned(
                    total, mapped(re, im), 0,
                    lambda c: (c // 2 * 2 + s1) * 8 + c % 2 * 4 + s3 * 2 + c2,
                )
        for c in range(4):
            re, im = finish(*total[c], 1)
            state[0, 2 * c + c2, 0] = re
            state[0, 2 * c + c2, 1] = im

    @pl.loop(0, 4, unroll=2)
    def _(c):
        total = [None] * 4
        for s2 in range(2):
            add_turned(
                total, mapped(state[0, 2 * c + s2, 0], state[0, 2 * c + s2, 1]), 1,
                lambda d: (c // 2 * 2 + d // 2) * 8 + c % 2 * 4 + d % 2 * 2 + s2,
            )
        low = lane_bit((K, LANES), 64)
        for d3 in range(2):
            re, im = finish(*(
                jnp.where(low, a + pltpu.roll(a, 64, 1), b + pltpu.roll(b, 64, 1))
                for a, b in zip(total[d3], total[2 + d3])
            ), 2)
            state[1, 2 * c + d3, 0] = re
            state[1, 2 * c + d3, 1] = im

    def gather_copy(slot):
        return pltpu.make_async_remote_copy(
            send_b.at[slot], recv_b.at[slot // 4, slot % 4], b_send, b_recv.at[slot // 4],
            device_id=gather_device(slot), device_id_type=MESH,
        )

    for r4 in range(2):
        for r3 in range(2):
            d4, d3 = flip(y4, r4), flip(y3, r3)
            total = [None] * 4
            for s in range(2):
                n = 4 * s + 2 * d4 + d3
                add_turned(
                    total, mapped(state[1, n, 0], state[1, n, 1]), 2,
                    lambda c: (s * 2 + c // 2) * 8 + 4 * d4 + 2 * d3 + c % 2,
                )
            low = lane_bit((K, LANES), 32)
            for c2 in range(2):
                re, im = finish(*(
                    jnp.where(low, a + pltpu.roll(a, 96, 1), b + pltpu.roll(b, 32, 1))
                    for a, b in zip(total[c2], total[2 + c2])
                ), 3)
                parts = pack(re, im)
                for e1 in range(2):
                    for e0 in range(2):
                        slot = 16 * r4 + 8 * flip(x0, e0) + 4 * flip(y2, c2) + 2 * flip(x1, e1) + r3
                        send_b[slot] = parts[2 * e1 + e0]
            for slot in range(32):
                if slot // 16 == r4 and slot % 2 == r3:
                    if slot == 0:
                        recv_b[0, 0] = send_b[0]
                    else:
                        gather_copy(slot).start()

    def z_copy(i):
        return pltpu.make_async_remote_copy(
            recv_b.at[i], recv_z.at[i], z_send, z_recv.at[i],
            device_id=partner_z, device_id_type=MESH,
        )

    def x_copy(i):
        return pltpu.make_async_remote_copy(
            recv_b.at[i] if i < 8 else recv_z.at[i - 8], recv_x.at[i], x_send, x_recv.at[i],
            device_id=partner_x, device_id_type=MESH,
        )

    def result_copy(block):
        return pltpu.make_async_copy(staged.at[block], out.at[:, :, block, :], out_sem)

    def expand(*blocks):
        places, parents = [], []
        for fx, fz, i in blocks:
            source = recv_x.at[8 * fz + i] if fx else recv_z.at[i] if fz else recv_b.at[i]
            places.append(
                16 * flip(x2, fx) + 8 * flip(y4, i // 4) + 4 * flip(y2, i % 2)
                + 2 * flip(flip(y1, fz), i % 2) + flip(x0, i // 2 % 2)
            )
            parents.append(split_rows(*unpack([source[flip_bits(group, g, 2)] for g in range(4)])))
        values = jnp.dot(own_map[...], jnp.concatenate(parents, 1), preferred_element_type=F32)
        for n, block in enumerate(places):
            re, im = (values[:, (2 * n + c) * LANES:(2 * n + c + 1) * LANES] for c in range(2))
            staged[block, 0], staged[block, 1] = turn(re, im, last[block, 0], last[block, 1])
            result_copy(block).start()

    def pair(fx, fz, n):
        expand(*((fx, fz, i) for i in GATHER_ORDER[n - 1:n + 1]))

    for n in range(8 + BEHIND):
        if n < 8:
            i = GATHER_ORDER[n]
            arrived = recv_b.at[0, pl.ds(1, 3)] if i == 0 else recv_b.at[i]
            pltpu.make_async_remote_copy(
                arrived, arrived, b_send, b_recv.at[i], device_id=partner_x, device_id_type=MESH
            ).wait_recv()
            z_copy(i).start()
            x_copy(i).start()
            if n % 2:
                pair(0, 0, n)
        m = n - BEHIND
        if m >= 0:
            z_copy(GATHER_ORDER[m]).wait_recv()
            x_copy(8 + GATHER_ORDER[m]).start()
            if m % 2:
                pair(0, 1, m)
    for n in range(1, 8, 2):
        for i in GATHER_ORDER[n - 1:n + 1]:
            x_copy(i).wait_recv()
        pair(1, 0, n)
    for n in range(1, 8, 2):
        for i in GATHER_ORDER[n - 1:n + 1]:
            x_copy(8 + i).wait_recv()
        pair(1, 1, n)

    for sent, sem in (
        (first, first_send), (second, second_send), (send_a.at[pl.ds(1, 31)], a_send),
        (send_b.at[pl.ds(1, 31)], b_send), (recv_z, z_send), (recv_x, x_send),
    ):
        pltpu.make_async_remote_copy(
            sent, sent, sem, a_recv, device_id=partner_x, device_id_type=MESH
        ).wait_send()
    pltpu.make_async_copy(staged, staged, out_sem).wait()


def per_device(coeff, phase_x, phase_y, phase_q, interp):
    field = (2, K, LANES)
    message = (32, LANES)
    dma = pltpu.SemaphoreType.DMA
    result = pl.pallas_call(
        kernel,
        out_shape=jax.ShapeDtypeStruct((2, K, 32, LANES), F32),
        in_specs=[
            pl.BlockSpec(memory_space=pltpu.HBM),
            pl.BlockSpec(memory_space=pltpu.HBM),
            pl.BlockSpec(memory_space=pltpu.HBM),
            pl.BlockSpec(memory_space=pltpu.HBM),
            pl.BlockSpec(memory_space=pltpu.HBM),
        ],
        out_specs=pl.BlockSpec(memory_space=pltpu.VMEM),
        scratch_shapes=[
            pltpu.VMEM((4, 2, 8, K), F32),
            pltpu.VMEM((4, 2, 32, K), F32),
            pltpu.VMEM((4, K, K), F32),
            pltpu.VMEM((8, 2, 2, *field), F32),
            pltpu.VMEM((8, 2, *field), F32),
            pltpu.VMEM((8, *field), F32),
            pltpu.VMEM((32, *message), F32),
            pltpu.VMEM((32, *message), F32),
            pltpu.VMEM((32, *message), F32),
            pltpu.VMEM((8, 4, *message), F32),
            pltpu.VMEM((8, 4, *message), F32),
            pltpu.VMEM((16, 4, *message), F32),
            pltpu.VMEM((2, 8, *field), F32),
            pltpu.VMEM((3, 4, LANES, LANES), F32),
            pltpu.VMEM((3, 8, LANES, LANES), F32),
            pltpu.VMEM((3, 32, LANES, LANES), F32),
            pltpu.VMEM((3, 8, K), F32),
            pltpu.VMEM((3, 8, K), F32),
            pltpu.VMEM((3, 32, K), F32),
            pltpu.VMEM((3, 32, K), F32),
            pltpu.VMEM((4, 2, K, LANES), F32),
            pltpu.VMEM((4, K, LANES), F32),
            pltpu.VMEM((4, K, LANES), F32),
            pltpu.VMEM((32, *field), F32),
            pltpu.VMEM((K, 32 * LANES), F32),
            pltpu.VMEM((32, *field), F32),
            pltpu.VMEM((4 * K, 3 * K), BF16),
            pltpu.VMEM((K, 3 * K), BF16),
            dma((3,)), dma((8,)), dma((2,)), dma, dma((8,)), dma, dma((8,)),
            dma, dma, dma, dma((8,)), dma, dma((8,)), dma, dma((16,)), dma,
        ],
        compiler_params=pltpu.CompilerParams(
            collective_id=0, has_side_effects=True, vmem_limit_bytes=60 * 1024 * 1024
        ),
    )(
        coeff.reshape(2, K, 32, LANES),
        phase_x.transpose(0, 1, 3, 2),
        phase_y.transpose(0, 1, 3, 2),
        phase_q,
        interp,
    )
    return result.reshape(2, K, 1, 1, 32 * LANES)


def solution(mesh):
    placed = (P(None, None, "gx", "gy", None), P(), P(), P(), P())
    return jax.shard_map(
        per_device,
        mesh=mesh,
        in_specs=placed,
        out_specs=P(None, None, "gx", "gy", None),
        check_vma=False,
    )
```

```python
import jax
import jax.numpy as jnp
import numpy as np
from jax import lax
from jax.experimental import pallas as pl
from jax.experimental.pallas import tpu as pltpu
from jax.sharding import PartitionSpec as P

MESH = pl.DeviceIdType.MESH
F32 = jnp.float32
BF16 = jnp.bfloat16
K = 64
LANES = 128
ORDER = (4, 5, 6, 7, 2, 3, 1, 0)
AHEAD = 4
LAG = 3
BEHIND = 3
GATHER_ORDER = (0, 2, 3, 1, 4, 6, 7, 5)


def flip(bit, other):
    return bit + other - 2 * bit * other


def flip_bits(value, mask, bits):
    total = 0
    for n in range(bits):
        total = total + (1 << n) * flip(value // (1 << n) % 2, mask // (1 << n) % 2)
    return total


def lane_bit(shape, width):
    return lax.broadcasted_iota(jnp.int32, shape, len(shape) - 1) // width % 2 == 0


def lane_transpose(parts):
    low64 = lane_bit(parts[0].shape, 64)
    low32 = lane_bit(parts[0].shape, 32)
    a, b, c, d = parts
    a, c = jnp.where(low64, a, pltpu.roll(c, 64, 1)), jnp.where(low64, pltpu.roll(a, 64, 1), c)
    b, d = jnp.where(low64, b, pltpu.roll(d, 64, 1)), jnp.where(low64, pltpu.roll(b, 64, 1), d)
    a, b = jnp.where(low32, a, pltpu.roll(b, 32, 1)), jnp.where(low32, pltpu.roll(a, 96, 1), b)
    c, d = jnp.where(low32, c, pltpu.roll(d, 32, 1)), jnp.where(low32, pltpu.roll(c, 96, 1), d)
    return a, b, c, d


def pack(re, im):
    return lane_transpose((re[:32], re[32:], im[:32], im[32:]))


def unpack(parts):
    a, b, c, d = lane_transpose(parts)
    return jnp.concatenate([a, b], 0), jnp.concatenate([c, d], 0)


def cos_sin(angle):
    turns = jnp.round(angle * (2 / np.pi))
    rest = angle - turns * 1.5703125
    rest = rest - turns * 4.837512969970703125e-4
    rest = rest - turns * 7.54978995489188216e-8
    square = rest * rest
    sine = rest + rest * square * (
        -1.6666654611e-1 + square * (8.3321608736e-3 + square * -1.9515295891e-4)
    )
    cosine = 1.0 - 0.5 * square + square * square * (
        4.166664568298827e-2 + square * (-1.388731625493765e-3 + square * 2.443315711809948e-5)
    )
    quarter = turns.astype(jnp.int32) & 3
    odd = (quarter & 1) == 1
    cos, sin = jnp.where(odd, sine, cosine), jnp.where(odd, cosine, sine)
    cos = jnp.where((quarter == 1) | (quarter == 2), -cos, cos)
    return cos, jnp.where(quarter >= 2, -sin, sin)


def turn(re, im, cos, sin):
    return re * cos - im * sin, re * sin + im * cos


def split_rows(re, im):
    both = jnp.concatenate([re, im], 1)
    high = both.astype(BF16)
    low = (both - high.astype(F32)).astype(BF16)
    return jnp.concatenate([high, low, high], 0)


def split_columns(blocks):
    high = blocks.astype(BF16).astype(F32)
    low = blocks - high
    return jnp.concatenate([high, high, low], 1).astype(BF16)


def kernel(
    coeff, small, phase_q, out,
    phase_x, phase_y, interp, field, first, second, send_a, recv_a, send_b, recv_b, recv_z, recv_x,
    partial, state, factor_x, factor_y, factor, x_cos, x_sin, y_cos, y_sin, q_own, q_cos, q_sin, last, q_last, staged,
    maps, own_map,
    small_sem, field_sem, q_sem, first_send, first_recv, second_send, second_recv,
    a_send, a_recv, b_send, b_recv, z_send, z_recv, x_send, x_recv, out_sem,
):
    gx, gy = lax.axis_index("gx"), lax.axis_index("gy")
    x2, x1, x0 = gx // 4, gx // 2 % 2, gx % 2
    y4, y3, y2, y1, core = gy // 16, gy // 8 % 2, gy // 4 % 2, gy // 2 % 2, gy % 2
    z = 4 * y2 + 2 * y1 + x0
    group = 2 * x1 + y3

    def device(fx2=0, fx1=0, fx0=0, fy4=0, fy3=0, fy2=0, fy1=0):
        return (
            4 * flip(x2, fx2) + 2 * flip(x1, fx1) + flip(x0, fx0),
            16 * flip(y4, fy4) + 8 * flip(y3, fy3) + 4 * flip(y2, fy2) + 2 * flip(y1, fy1) + core,
        )

    def spread_device(slot):
        return device(
            fy2=slot // 16, fy1=slot // 8 % 2, fx0=slot // 4 % 2, fx1=slot // 2 % 2, fy3=slot % 2
        )

    def gather_device(slot):
        return device(
            fy4=slot // 16, fx0=slot // 8 % 2, fy2=slot // 4 % 2, fy1=slot // 4 % 2,
            fx1=slot // 2 % 2, fy3=slot % 2,
        )

    barrier = pltpu.get_barrier_semaphore()
    for slot in range(1, 32):
        pl.semaphore_signal(barrier, inc=1, device_id=spread_device(slot), device_id_type=MESH)
    for slot in range(16, 32):
        pl.semaphore_signal(barrier, inc=1, device_id=gather_device(slot), device_id_type=MESH)
    pl.semaphore_signal(barrier, inc=1, device_id=device(fx2=1), device_id_type=MESH)

    def load(i):
        for fx in range(2):
            for fy in range(2):
                block = 16 * flip(x2, fx) + 8 * flip(y4, fy) + flip_bits(z, i, 3)
                yield pltpu.make_async_copy(
                    coeff.at[:, :, block, :], field.at[i, fx, fy], field_sem.at[i]
                )

    small_copies = [
        pltpu.make_async_copy(small.at[:, :, pl.ds(first_row, rows), :], target, small_sem.at[n])
        for n, (first_row, rows, target) in enumerate(
            ((0, 8, phase_x), (8, 32, phase_y), (40, 32, interp))
        )
    ]
    for copy in small_copies:
        copy.start()
    for i in ORDER:
        for copy in load(i):
            copy.start()
    own_block = 16 * x2 + 8 * y4 + z
    own_copy = pltpu.make_async_copy(
        phase_q.at[:, :, :, pl.ds(pl.multiple_of(own_block * LANES, LANES), LANES)], q_own, q_sem.at[0]
    )
    own_copy.start()
    last_copy = pltpu.make_async_copy(phase_q.at[3, 1], q_last, q_sem.at[1])
    last_copy.start()

    def columns(row):
        wide = jnp.broadcast_to(jnp.concatenate([row, row], 1), (LANES, LANES))
        return wide.T[:K]

    for copy in small_copies:
        copy.wait()
    angle = phase_x[0, 0, pl.ds(gx, 1), :] + phase_y[0, 0, pl.ds(gy, 1), :]
    in_cos, in_sin = (columns(part) for part in cos_sin(-angle))
    out_angle = columns(phase_x[3, 1, pl.ds(gx, 1), :] + phase_y[3, 1, pl.ds(gy, 1), :])

    def rotate(i, fx, fy):
        re, im = turn(field[i, fx, fy, 0], field[i, fx, fy, 1], in_cos, in_sin)
        field[i, fx, fy, 0] = re
        field[i, fx, fy, 1] = im

    pl.semaphore_wait(barrier, 48)

    x_first = [ORDER.index(i) % 2 == 0 for i in range(8)]
    partner_x, partner_y, partner_z = device(fx2=1), device(fy4=1), device(fy1=1)

    def first_copy(i, c):
        return pltpu.make_async_remote_copy(
            field.at[i, 1, :, c] if x_first[i] else field.at[i, :, 1, c],
            first.at[i, :, c], first_send, first_recv.at[i, c],
            device_id=partner_x if x_first[i] else partner_y, device_id_type=MESH,
        )

    def second_copy(i, c):
        return pltpu.make_async_remote_copy(
            field.at[i, 0, 1, c] if x_first[i] else field.at[i, 1, 0, c],
            second.at[i, c], second_send, second_recv.at[i, c],
            device_id=partner_y if x_first[i] else partner_x, device_id_type=MESH,
        )

    def part_factors():
        for l in range(3):
            difference = phase_x[l, 1] - phase_x[l + 1, 0]
            x_cos[l], x_sin[l] = cos_sin(difference)
            difference = phase_y[l, 1] - phase_y[l + 1, 0]
            y_cos[l], y_sin[l] = cos_sin(difference)

    def edge_factors(l):
        def rows(cos, sin, places, count):
            return [
                jnp.broadcast_to(
                    jnp.concatenate([cos[l, pl.ds(p, 1), :], sin[l, pl.ds(p, 1), :]], 1), (count, LANES)
                )
                for p in places
            ]

        @pl.loop(0, 4, unroll=True)
        def _(n):
            places = [2 * n + h if l < 2 else n // 2 * 4 + h * 2 + n % 2 for h in range(2)]
            factor_x[l, n] = jnp.concatenate(rows(x_cos, x_sin, places, 64), 0).T

        @pl.loop(0, 8, unroll=True)
        def _(n):
            places = [4 * n + 2 * h + core for h in range(2)] * 2
            factor_y[l, n] = jnp.concatenate(rows(y_cos, y_sin, places, 32), 0).T

    def level_factors(l):
        @pl.loop(0, 32, unroll=4)
        def _(n):
            x, y = n // 8, n % 8
            cos, sin = turn(
                factor_x[l, x, :K], factor_x[l, x, K:], factor_y[l, y, :K], factor_y[l, y, K:]
            )
            factor[l, n, :K] = cos
            factor[l, n, K:] = sin

    def block_of(c):
        return jnp.concatenate([interp[c, 0], interp[c, 1]], 0)

    def small_factors():
        own_copy.wait()
        for l in range(4):
            value = -q_own[0, 0] if l == 0 else q_own[l - 1, 1] - q_own[l, 0]
            value = pltpu.roll(value, (128 - 32 * group) % 128, 1)
            value = jnp.where(lax.broadcasted_iota(jnp.int32, value.shape, 1) < 32, value, 0.0)
            value = value + pltpu.roll(value, 32, 1)
            value = value + pltpu.roll(value, 64, 1)
            q_cos[l], q_sin[l] = cos_sin(value)
        maps[...] = jnp.concatenate([split_columns(block_of(c)) for c in range(4)], 0)
        own_map[...] = split_columns(block_of(2 * x2 + y1))

    def last_factors():
        @pl.loop(0, 32, unroll=4)
        def _(block):
            value = out_angle + q_last[:, pl.ds(pl.multiple_of(block * LANES, LANES), LANES)]
            last[block, 0], last[block, 1] = cos_sin(value)

    def start_first(i):
        pltpu.make_async_copy(field.at[i], field.at[i], field_sem.at[i]).wait()
        for fx, fy in ((1, 1), (1, 0) if x_first[i] else (0, 1)):
            rotate(i, fx, fy)
        first_copy(i, 0).start()
        first_copy(i, 1).start()
        for fx, fy in ((0, 0), (0, 1) if x_first[i] else (1, 0)):
            rotate(i, fx, fy)

    def spread_copy(slot):
        return pltpu.make_async_remote_copy(
            send_a.at[slot], recv_a.at[slot], a_send, a_recv.at[slot // 16],
            device_id=spread_device(slot), device_id_type=MESH,
        )

    def start_second(i):
        fx, fy = (0, 1) if x_first[i] else (1, 0)
        for c in range(2):
            first_copy(i, c).wait_recv()
            field[i, fx, fy, c] = field[i, fx, fy, c] + first[i, 1, c]
            second_copy(i, c).start()
        field[i, 0, 0] = field[i, 0, 0] + first[i, 0]

    def spread(i):
        second_copy(i, 0).wait_recv()
        second_copy(i, 1).wait_recv()
        parts = pack(field[i, 0, 0, 0] + second[i, 0], field[i, 0, 0, 1] + second[i, 1])
        for g in range(4):
            send_a[4 * i + flip_bits(group, g, 2)] = parts[g]
        for g in range(4):
            if i == 0 and g == 0:
                recv_a[0] = send_a[0]
            else:
                spread_copy(4 * i + g).start()

    for i in ORDER[:AHEAD]:
        start_first(i)
    last_copy.wait()
    last_factors()
    part_factors()
    edge_factors(0)
    edge_factors(1)
    for n in range(8 + LAG):
        if n < 8:
            start_second(ORDER[n])
        if n + AHEAD < 8:
            start_first(ORDER[n + AHEAD])
        if n >= LAG:
            spread(ORDER[n - LAG])
        if n == 0:
            edge_factors(2)
        elif n < 4:
            level_factors(n - 1)
        elif n == 4:
            small_factors()

    def mapped(re, im):
        return jnp.dot(maps[...], split_rows(re, im), preferred_element_type=F32)

    def add_turned(total, values, l, place):
        for c in range(4):
            cos, sin = factor[l, place(c), :K], factor[l, place(c), K:]
            re, im = turn(values[c * K:(c + 1) * K, :LANES], values[c * K:(c + 1) * K, LANES:], cos, sin)
            total[c] = (re, im) if total[c] is None else (total[c][0] + re, total[c][1] + im)

    def finish(re, im, l):
        return turn(re, im, q_cos[l], q_sin[l])

    low = lane_bit((K, LANES), 64)
    for r2 in (1, 0):
        arrived = recv_a.at[pl.ds(16, 16)] if r2 else recv_a.at[pl.ds(1, 15)]
        pltpu.make_async_remote_copy(
            arrived, arrived, a_send, a_recv.at[r2], device_id=partner_x, device_id_type=MESH
        ).wait_recv()
        c2 = flip(y2, r2)
        total = [None] * 4
        for s1 in range(2):
            for s3 in range(2):
                messages = []
                for s0 in range(2):
                    for t1 in range(2):
                        place = 4 * r2 + 2 * flip(y1, t1) + flip(x0, s0)
                        messages.append(recv_a[4 * place + 2 * flip(x1, s1) + flip(y3, s3)])
                re, im = finish(*unpack(messages), 0)
                add_turned(
                    total, mapped(re, im), 0,
                    lambda c: (c // 2 * 2 + s1) * 8 + c % 2 * 4 + s3 * 2 + c2,
                )
        for c in range(4):
            parent = finish(*total[c], 1)
            children = [None] * 4
            if r2 == 0:
                children = [(partial[c, d, 0], partial[c, d, 1]) for d in range(4)]
            add_turned(
                children, mapped(*parent), 1,
                lambda d: (c // 2 * 2 + d // 2) * 8 + c % 2 * 4 + d % 2 * 2 + c2,
            )
            if r2 == 1:
                for d in range(4):
                    partial[c, d, 0], partial[c, d, 1] = children[d]
                continue
            for d3 in range(2):
                state[2 * c + d3, 0], state[2 * c + d3, 1] = finish(*(
                    jnp.where(low, a + pltpu.roll(a, 64, 1), b + pltpu.roll(b, 64, 1))
                    for a, b in zip(children[d3], children[2 + d3])
                ), 2)

    def gather_copy(slot):
        return pltpu.make_async_remote_copy(
            send_b.at[slot], recv_b.at[slot // 4, slot % 4], b_send, b_recv.at[slot // 4],
            device_id=gather_device(slot), device_id_type=MESH,
        )

    for r4 in range(2):
        for r3 in range(2):
            d4, d3 = flip(y4, r4), flip(y3, r3)
            total = [None] * 4
            for s in range(2):
                n = 4 * s + 2 * d4 + d3
                add_turned(
                    total, mapped(state[n, 0], state[n, 1]), 2,
                    lambda c: (s * 2 + c // 2) * 8 + 4 * d4 + 2 * d3 + c % 2,
                )
            low = lane_bit((K, LANES), 32)
            for c2 in range(2):
                re, im = finish(*(
                    jnp.where(low, a + pltpu.roll(a, 96, 1), b + pltpu.roll(b, 32, 1))
                    for a, b in zip(total[c2], total[2 + c2])
                ), 3)
                parts = pack(re, im)
                for e1 in range(2):
                    for e0 in range(2):
                        slot = 16 * r4 + 8 * flip(x0, e0) + 4 * flip(y2, c2) + 2 * flip(x1, e1) + r3
                        send_b[slot] = parts[2 * e1 + e0]
            for slot in range(32):
                if slot // 16 == r4 and slot % 2 == r3:
                    if slot == 0:
                        recv_b[0, 0] = send_b[0]
                    else:
                        gather_copy(slot).start()

    def z_copy(i):
        return pltpu.make_async_remote_copy(
            recv_b.at[i], recv_z.at[i], z_send, z_recv.at[i],
            device_id=partner_z, device_id_type=MESH,
        )

    def x_copy(i):
        return pltpu.make_async_remote_copy(
            recv_b.at[i] if i < 8 else recv_z.at[i - 8], recv_x.at[i], x_send, x_recv.at[i],
            device_id=partner_x, device_id_type=MESH,
        )

    def result_copy(block):
        return pltpu.make_async_copy(staged.at[block], out.at[:, :, block, :], out_sem)

    def expand(*blocks):
        places, parents = [], []
        for fx, fz, i in blocks:
            source = recv_x.at[8 * fz + i] if fx else recv_z.at[i] if fz else recv_b.at[i]
            places.append(
                16 * flip(x2, fx) + 8 * flip(y4, i // 4) + 4 * flip(y2, i % 2)
                + 2 * flip(flip(y1, fz), i % 2) + flip(x0, i // 2 % 2)
            )
            parents.append(split_rows(*unpack([source[flip_bits(group, g, 2)] for g in range(4)])))
        values = jnp.dot(own_map[...], jnp.concatenate(parents, 1), preferred_element_type=F32)
        for n, block in enumerate(places):
            re, im = (values[:, (2 * n + c) * LANES:(2 * n + c + 1) * LANES] for c in range(2))
            staged[block, 0], staged[block, 1] = turn(re, im, last[block, 0], last[block, 1])
            result_copy(block).start()

    def pair(fx, fz, n):
        expand(*((fx, fz, i) for i in GATHER_ORDER[n - 1:n + 1]))

    for n in range(8 + BEHIND):
        if n < 8:
            i = GATHER_ORDER[n]
            arrived = recv_b.at[0, pl.ds(1, 3)] if i == 0 else recv_b.at[i]
            pltpu.make_async_remote_copy(
                arrived, arrived, b_send, b_recv.at[i], device_id=partner_x, device_id_type=MESH
            ).wait_recv()
            z_copy(i).start()
            x_copy(i).start()
            if n % 2:
                pair(0, 0, n)
        m = n - BEHIND
        if m >= 0:
            z_copy(GATHER_ORDER[m]).wait_recv()
            x_copy(8 + GATHER_ORDER[m]).start()
            if m % 2:
                pair(0, 1, m)
    for n in range(1, 8, 2):
        for i in GATHER_ORDER[n - 1:n + 1]:
            x_copy(i).wait_recv()
        pair(1, 0, n)
    for n in range(1, 8, 2):
        for i in GATHER_ORDER[n - 1:n + 1]:
            x_copy(8 + i).wait_recv()
        pair(1, 1, n)

    for sent, sem in (
        (first, first_send), (second, second_send), (send_a.at[pl.ds(1, 31)], a_send),
        (send_b.at[pl.ds(1, 31)], b_send), (recv_z, z_send), (recv_x, x_send),
    ):
        pltpu.make_async_remote_copy(
            sent, sent, sem, a_recv.at[0], device_id=partner_x, device_id_type=MESH
        ).wait_send()
    pltpu.make_async_copy(staged, staged, out_sem).wait()


def per_device(coeff, phase_x, phase_y, phase_q, interp):
    field = (2, K, LANES)
    message = (32, LANES)
    dma = pltpu.SemaphoreType.DMA
    result = pl.pallas_call(
        kernel,
        out_shape=jax.ShapeDtypeStruct((2, K, 32, LANES), F32),
        in_specs=[
            pl.BlockSpec(memory_space=pl.ANY),
            pl.BlockSpec(memory_space=pl.ANY),
            pl.BlockSpec(memory_space=pl.ANY),
        ],
        out_specs=pl.BlockSpec(memory_space=pltpu.VMEM),
        scratch_shapes=[
            pltpu.VMEM((4, 2, 8, K), F32),
            pltpu.VMEM((4, 2, 32, K), F32),
            pltpu.VMEM((4, 2, 32, K), F32),
            pltpu.VMEM((8, 2, 2, *field), F32),
            pltpu.VMEM((8, 2, *field), F32),
            pltpu.VMEM((8, *field), F32),
            pltpu.VMEM((32, *message), F32),
            pltpu.VMEM((32, *message), F32),
            pltpu.VMEM((32, *message), F32),
            pltpu.VMEM((8, 4, *message), F32),
            pltpu.VMEM((8, 4, *message), F32),
            pltpu.VMEM((16, 4, *message), F32),
            pltpu.VMEM((4, 4, *field), F32),
            pltpu.VMEM((8, *field), F32),
            pltpu.VMEM((3, 4, LANES, LANES), F32),
            pltpu.VMEM((3, 8, LANES, LANES), F32),
            pltpu.VMEM((3, 32, LANES, LANES), F32),
            pltpu.VMEM((3, 8, K), F32),
            pltpu.VMEM((3, 8, K), F32),
            pltpu.VMEM((3, 32, K), F32),
            pltpu.VMEM((3, 32, K), F32),
            pltpu.VMEM((4, 2, K, LANES), F32),
            pltpu.VMEM((4, K, LANES), F32),
            pltpu.VMEM((4, K, LANES), F32),
            pltpu.VMEM((32, *field), F32),
            pltpu.VMEM((K, 32 * LANES), F32),
            pltpu.VMEM((32, *field), F32),
            pltpu.VMEM((4 * K, 3 * K), BF16),
            pltpu.VMEM((K, 3 * K), BF16),
            dma((3,)), dma((8,)), dma((2,)), dma, dma((8, 2)), dma, dma((8, 2)),
            dma, dma((2,)), dma, dma((8,)), dma, dma((8,)), dma, dma((16,)), dma,
        ],
        compiler_params=pltpu.CompilerParams(
            collective_id=0, has_side_effects=True, vmem_limit_bytes=51 * 1024 * 1024
        ),
    )(
        coeff.reshape(2, K, 32, LANES),
        jnp.concatenate(
            [phase_x.transpose(0, 1, 3, 2), phase_y.transpose(0, 1, 3, 2), interp.reshape(4, 2, 32, K)], 2
        ),
        phase_q,
    )
    return result.reshape(2, K, 1, 1, 32 * LANES)


def solution(mesh):
    placed = (P(None, None, "gx", "gy", None), P(), P(), P(), P())
    return jax.shard_map(
        per_device,
        mesh=mesh,
        in_specs=placed,
        out_specs=P(None, None, "gx", "gy", None),
        check_vma=False,
    )
```

```python
import jax
import jax.numpy as jnp
import numpy as np
from jax import lax
from jax.experimental import pallas as pl
from jax.experimental.pallas import tpu as pltpu
from jax.sharding import PartitionSpec as P

MESH = pl.DeviceIdType.MESH
F32 = jnp.float32
BF16 = jnp.bfloat16
K = 64
LANES = 128
ORDER = (4, 5, 6, 7, 3, 2, 1, 0)
AHEAD = 4
LAG = 3
BEHIND = 3
GATHER_ORDER = (0, 2, 3, 1, 4, 6, 7, 5)


def flip(bit, other):
    return bit + other - 2 * bit * other


def flip_bits(value, mask, bits):
    total = 0
    for n in range(bits):
        total = total + (1 << n) * flip(value // (1 << n) % 2, mask // (1 << n) % 2)
    return total


def lane_bit(shape, width):
    return lax.broadcasted_iota(jnp.int32, shape, len(shape) - 1) // width % 2 == 0


def lane_transpose(parts):
    low64 = lane_bit(parts[0].shape, 64)
    low32 = lane_bit(parts[0].shape, 32)
    a, b, c, d = parts
    a, c = jnp.where(low64, a, pltpu.roll(c, 64, 1)), jnp.where(low64, pltpu.roll(a, 64, 1), c)
    b, d = jnp.where(low64, b, pltpu.roll(d, 64, 1)), jnp.where(low64, pltpu.roll(b, 64, 1), d)
    a, b = jnp.where(low32, a, pltpu.roll(b, 32, 1)), jnp.where(low32, pltpu.roll(a, 96, 1), b)
    c, d = jnp.where(low32, c, pltpu.roll(d, 32, 1)), jnp.where(low32, pltpu.roll(c, 96, 1), d)
    return a, b, c, d


def pack(re, im):
    return lane_transpose((re[:32], re[32:], im[:32], im[32:]))


def unpack(parts):
    a, b, c, d = lane_transpose(parts)
    return jnp.concatenate([a, b], 0), jnp.concatenate([c, d], 0)


def cos_sin(angle):
    turns = jnp.round(angle * (2 / np.pi))
    rest = angle - turns * 1.5703125
    rest = rest - turns * 4.837512969970703125e-4
    rest = rest - turns * 7.54978995489188216e-8
    square = rest * rest
    sine = rest + rest * square * (
        -1.6666654611e-1 + square * (8.3321608736e-3 + square * -1.9515295891e-4)
    )
    cosine = 1.0 - 0.5 * square + square * square * (
        4.166664568298827e-2 + square * (-1.388731625493765e-3 + square * 2.443315711809948e-5)
    )
    quarter = turns.astype(jnp.int32) & 3
    odd = (quarter & 1) == 1
    cos, sin = jnp.where(odd, sine, cosine), jnp.where(odd, cosine, sine)
    cos = jnp.where((quarter == 1) | (quarter == 2), -cos, cos)
    return cos, jnp.where(quarter >= 2, -sin, sin)


def turn(re, im, cos, sin):
    return re * cos - im * sin, re * sin + im * cos


def split_rows(re, im):
    both = jnp.concatenate([re, im], 1)
    high = both.astype(BF16)
    low = (both - high.astype(F32)).astype(BF16)
    return jnp.concatenate([high, low, high], 0)


def split_columns(blocks):
    high = blocks.astype(BF16).astype(F32)
    low = blocks - high
    return jnp.concatenate([high, high, low], 1).astype(BF16)


def kernel(
    coeff, small, phase_q, out,
    phase_x, phase_y, interp, field, first, second, send_a, recv_a, send_b, recv_b, recv_z, recv_x,
    partial, state, factor_x, factor_y, factor, x_cos, x_sin, y_cos, y_sin, q_own, q_cos, q_sin, last, q_last, staged,
    maps, own_map,
    small_sem, field_sem, q_sem, first_send, first_recv, second_send, second_recv,
    a_send, a_recv, b_send, b_recv, z_send, z_recv, x_send, x_recv, out_sem,
):
    gx, gy = lax.axis_index("gx"), lax.axis_index("gy")
    x2, x1, x0 = gx // 4, gx // 2 % 2, gx % 2
    y4, y3, y2, y1, core = gy // 16, gy // 8 % 2, gy // 4 % 2, gy // 2 % 2, gy % 2
    z = 4 * y2 + 2 * y1 + x0
    group = 2 * x1 + y3

    def device(fx2=0, fx1=0, fx0=0, fy4=0, fy3=0, fy2=0, fy1=0):
        return (
            4 * flip(x2, fx2) + 2 * flip(x1, fx1) + flip(x0, fx0),
            16 * flip(y4, fy4) + 8 * flip(y3, fy3) + 4 * flip(y2, fy2) + 2 * flip(y1, fy1) + core,
        )

    def spread_device(slot):
        return device(
            fy2=slot // 16, fy1=slot // 8 % 2, fx0=slot // 4 % 2, fx1=slot // 2 % 2, fy3=slot % 2
        )

    def gather_device(slot):
        return device(
            fy4=slot // 16, fx0=slot // 8 % 2, fy2=slot // 4 % 2, fy1=slot // 4 % 2,
            fx1=slot // 2 % 2, fy3=slot % 2,
        )

    barrier = pltpu.get_barrier_semaphore()
    for slot in range(1, 32):
        pl.semaphore_signal(barrier, inc=1, device_id=spread_device(slot), device_id_type=MESH)
    for slot in range(16, 32):
        pl.semaphore_signal(barrier, inc=1, device_id=gather_device(slot), device_id_type=MESH)
    pl.semaphore_signal(barrier, inc=1, device_id=device(fx2=1), device_id_type=MESH)

    def load(i):
        for fx in range(2):
            for fy in range(2):
                block = 16 * flip(x2, fx) + 8 * flip(y4, fy) + flip_bits(z, i, 3)
                yield pltpu.make_async_copy(
                    coeff.at[:, :, block, :], field.at[i, fx, fy], field_sem.at[i]
                )

    small_copies = [
        pltpu.make_async_copy(small.at[:, :, pl.ds(first_row, rows), :], target, small_sem.at[n])
        for n, (first_row, rows, target) in enumerate(
            ((0, 8, phase_x), (8, 32, phase_y), (40, 32, interp))
        )
    ]
    for copy in small_copies:
        copy.start()
    for i in ORDER:
        for copy in load(i):
            copy.start()
    own_block = 16 * x2 + 8 * y4 + z
    own_copy = pltpu.make_async_copy(
        phase_q.at[:, :, :, pl.ds(pl.multiple_of(own_block * LANES, LANES), LANES)], q_own, q_sem.at[0]
    )
    own_copy.start()
    last_copy = pltpu.make_async_copy(phase_q.at[3, 1], q_last, q_sem.at[1])
    last_copy.start()

    def columns(row):
        wide = jnp.broadcast_to(jnp.concatenate([row, row], 1), (LANES, LANES))
        return wide.T[:K]

    for copy in small_copies:
        copy.wait()
    angle = phase_x[0, 0, pl.ds(gx, 1), :] + phase_y[0, 0, pl.ds(gy, 1), :]
    in_cos, in_sin = (columns(part) for part in cos_sin(-angle))
    out_angle = columns(phase_x[3, 1, pl.ds(gx, 1), :] + phase_y[3, 1, pl.ds(gy, 1), :])

    def rotate(i, fx, fy):
        re, im = turn(field[i, fx, fy, 0], field[i, fx, fy, 1], in_cos, in_sin)
        field[i, fx, fy, 0] = re
        field[i, fx, fy, 1] = im

    pl.semaphore_wait(barrier, 48)

    x_first = [ORDER.index(i) % 2 == 0 for i in range(8)]
    partner_x, partner_y, partner_z = device(fx2=1), device(fy4=1), device(fy1=1)

    def first_copy(i, c):
        return pltpu.make_async_remote_copy(
            field.at[i, 1, :, c] if x_first[i] else field.at[i, :, 1, c],
            first.at[i, :, c], first_send, first_recv.at[i, c],
            device_id=partner_x if x_first[i] else partner_y, device_id_type=MESH,
        )

    def second_copy(i, c):
        return pltpu.make_async_remote_copy(
            field.at[i, 0, 1, c] if x_first[i] else field.at[i, 1, 0, c],
            second.at[i, c], second_send, second_recv.at[i, c],
            device_id=partner_y if x_first[i] else partner_x, device_id_type=MESH,
        )

    def part_factors():
        for l in range(3):
            difference = phase_x[l, 1] - phase_x[l + 1, 0]
            x_cos[l], x_sin[l] = cos_sin(difference)
            difference = phase_y[l, 1] - phase_y[l + 1, 0]
            y_cos[l], y_sin[l] = cos_sin(difference)

    def edge_factors(l):
        def rows(cos, sin, places, count):
            return [
                jnp.broadcast_to(
                    jnp.concatenate([cos[l, pl.ds(p, 1), :], sin[l, pl.ds(p, 1), :]], 1), (count, LANES)
                )
                for p in places
            ]

        @pl.loop(0, 4, unroll=True)
        def _(n):
            places = [2 * n + h if l < 2 else n // 2 * 4 + h * 2 + n % 2 for h in range(2)]
            factor_x[l, n] = jnp.concatenate(rows(x_cos, x_sin, places, 64), 0).T

        @pl.loop(0, 8, unroll=True)
        def _(n):
            places = [4 * n + 2 * h + core for h in range(2)] * 2
            factor_y[l, n] = jnp.concatenate(rows(y_cos, y_sin, places, 32), 0).T

    def level_factors(l):
        @pl.loop(0, 32, unroll=4)
        def _(n):
            x, y = n // 8, n % 8
            cos, sin = turn(
                factor_x[l, x, :K], factor_x[l, x, K:], factor_y[l, y, :K], factor_y[l, y, K:]
            )
            factor[l, n, :K] = cos
            factor[l, n, K:] = sin

    def block_of(c):
        return jnp.concatenate([interp[c, 0], interp[c, 1]], 0)

    def small_factors():
        own_copy.wait()
        for l in range(4):
            value = -q_own[0, 0] if l == 0 else q_own[l - 1, 1] - q_own[l, 0]
            value = pltpu.roll(value, (128 - 32 * group) % 128, 1)
            value = jnp.where(lax.broadcasted_iota(jnp.int32, value.shape, 1) < 32, value, 0.0)
            value = value + pltpu.roll(value, 32, 1)
            value = value + pltpu.roll(value, 64, 1)
            q_cos[l], q_sin[l] = cos_sin(value)
        maps[...] = jnp.concatenate([split_columns(block_of(c)) for c in range(4)], 0)
        own_map[...] = split_columns(block_of(2 * x2 + y1))

    def last_factors():
        @pl.loop(0, 32, unroll=4)
        def _(block):
            value = out_angle + q_last[:, pl.ds(pl.multiple_of(block * LANES, LANES), LANES)]
            last[block, 0], last[block, 1] = cos_sin(value)

    def start_first(i):
        pltpu.make_async_copy(field.at[i], field.at[i], field_sem.at[i]).wait()
        for fx, fy in ((1, 1), (1, 0) if x_first[i] else (0, 1)):
            rotate(i, fx, fy)
        first_copy(i, 0).start()
        first_copy(i, 1).start()
        for fx, fy in ((0, 0), (0, 1) if x_first[i] else (1, 0)):
            rotate(i, fx, fy)

    def spread_copy(slot):
        return pltpu.make_async_remote_copy(
            send_a.at[slot], recv_a.at[slot], a_send, a_recv.at[slot // 16],
            device_id=spread_device(slot), device_id_type=MESH,
        )

    def start_second(i):
        fx, fy = (0, 1) if x_first[i] else (1, 0)
        for c in range(2):
            first_copy(i, c).wait_recv()
            field[i, fx, fy, c] = field[i, fx, fy, c] + first[i, 1, c]
            second_copy(i, c).start()
        field[i, 0, 0] = field[i, 0, 0] + first[i, 0]

    def spread(i):
        second_copy(i, 0).wait_recv()
        second_copy(i, 1).wait_recv()
        parts = pack(field[i, 0, 0, 0] + second[i, 0], field[i, 0, 0, 1] + second[i, 1])
        for g in range(4):
            send_a[4 * i + flip_bits(group, g, 2)] = parts[g]
        for g in range(4):
            if i == 0 and g == 0:
                recv_a[0] = send_a[0]
            else:
                spread_copy(4 * i + g).start()

    for i in ORDER[:AHEAD]:
        start_first(i)
    last_copy.wait()
    last_factors()
    part_factors()
    edge_factors(0)
    edge_factors(1)
    for n in range(8 + LAG):
        if n < 8:
            start_second(ORDER[n])
        if n + AHEAD < 8:
            start_first(ORDER[n + AHEAD])
        if n >= LAG:
            spread(ORDER[n - LAG])
        if n == 0:
            edge_factors(2)
        elif n < 4:
            level_factors(n - 1)
        elif n == 4:
            small_factors()

    def mapped(re, im):
        return jnp.dot(maps[...], split_rows(re, im), preferred_element_type=F32)

    def add_turned(total, values, l, place):
        for c in range(4):
            cos, sin = factor[l, place(c), :K], factor[l, place(c), K:]
            re, im = turn(values[c * K:(c + 1) * K, :LANES], values[c * K:(c + 1) * K, LANES:], cos, sin)
            total[c] = (re, im) if total[c] is None else (total[c][0] + re, total[c][1] + im)

    def finish(re, im, l):
        return turn(re, im, q_cos[l], q_sin[l])

    low = lane_bit((K, LANES), 64)
    for r2 in (1, 0):
        arrived = recv_a.at[pl.ds(16, 16)] if r2 else recv_a.at[pl.ds(1, 15)]
        pltpu.make_async_remote_copy(
            arrived, arrived, a_send, a_recv.at[r2], device_id=partner_x, device_id_type=MESH
        ).wait_recv()
        c2 = flip(y2, r2)
        total = [None] * 4
        for s1 in range(2):
            for s3 in range(2):
                messages = []
                for s0 in range(2):
                    for t1 in range(2):
                        place = 4 * r2 + 2 * flip(y1, t1) + flip(x0, s0)
                        messages.append(recv_a[4 * place + 2 * flip(x1, s1) + flip(y3, s3)])
                re, im = finish(*unpack(messages), 0)
                add_turned(
                    total, mapped(re, im), 0,
                    lambda c: (c // 2 * 2 + s1) * 8 + c % 2 * 4 + s3 * 2 + c2,
                )
        for c in range(4):
            parent = finish(*total[c], 1)
            children = [None] * 4
            if r2 == 0:
                children = [(partial[c, d, 0], partial[c, d, 1]) for d in range(4)]
            add_turned(
                children, mapped(*parent), 1,
                lambda d: (c // 2 * 2 + d // 2) * 8 + c % 2 * 4 + d % 2 * 2 + c2,
            )
            if r2 == 1:
                for d in range(4):
                    partial[c, d, 0], partial[c, d, 1] = children[d]
                continue
            for d3 in range(2):
                state[2 * c + d3, 0], state[2 * c + d3, 1] = finish(*(
                    jnp.where(low, a + pltpu.roll(a, 64, 1), b + pltpu.roll(b, 64, 1))
                    for a, b in zip(children[d3], children[2 + d3])
                ), 2)

    def gather_copy(slot):
        return pltpu.make_async_remote_copy(
            send_b.at[slot], recv_b.at[slot // 4, slot % 4], b_send, b_recv.at[slot // 4],
            device_id=gather_device(slot), device_id_type=MESH,
        )

    for r4 in range(2):
        for r3 in range(2):
            d4, d3 = flip(y4, r4), flip(y3, r3)
            total = [None] * 4
            for s in range(2):
                n = 4 * s + 2 * d4 + d3
                add_turned(
                    total, mapped(state[n, 0], state[n, 1]), 2,
                    lambda c: (s * 2 + c // 2) * 8 + 4 * d4 + 2 * d3 + c % 2,
                )
            low = lane_bit((K, LANES), 32)
            for c2 in range(2):
                re, im = finish(*(
                    jnp.where(low, a + pltpu.roll(a, 96, 1), b + pltpu.roll(b, 32, 1))
                    for a, b in zip(total[c2], total[2 + c2])
                ), 3)
                parts = pack(re, im)
                for e1 in range(2):
                    for e0 in range(2):
                        slot = 16 * r4 + 8 * flip(x0, e0) + 4 * flip(y2, c2) + 2 * flip(x1, e1) + r3
                        send_b[slot] = parts[2 * e1 + e0]
            for slot in range(32):
                if slot // 16 == r4 and slot % 2 == r3:
                    if slot == 0:
                        recv_b[0, 0] = send_b[0]
                    else:
                        gather_copy(slot).start()

    def z_copy(i):
        return pltpu.make_async_remote_copy(
            recv_b.at[i], recv_z.at[i], z_send, z_recv.at[i],
            device_id=partner_z, device_id_type=MESH,
        )

    def x_copy(i):
        return pltpu.make_async_remote_copy(
            recv_b.at[i] if i < 8 else recv_z.at[i - 8], recv_x.at[i], x_send, x_recv.at[i],
            device_id=partner_x, device_id_type=MESH,
        )

    def result_copy(block):
        return pltpu.make_async_copy(staged.at[block], out.at[:, :, block, :], out_sem)

    def expand(*blocks):
        places, parents = [], []
        for fx, fz, i in blocks:
            source = recv_x.at[8 * fz + i] if fx else recv_z.at[i] if fz else recv_b.at[i]
            places.append(
                16 * flip(x2, fx) + 8 * flip(y4, i // 4) + 4 * flip(y2, i % 2)
                + 2 * flip(flip(y1, fz), i % 2) + flip(x0, i // 2 % 2)
            )
            parents.append(split_rows(*unpack([source[flip_bits(group, g, 2)] for g in range(4)])))
        values = jnp.dot(own_map[...], jnp.concatenate(parents, 1), preferred_element_type=F32)
        for n, block in enumerate(places):
            re, im = (values[:, (2 * n + c) * LANES:(2 * n + c + 1) * LANES] for c in range(2))
            staged[block, 0], staged[block, 1] = turn(re, im, last[block, 0], last[block, 1])
            result_copy(block).start()

    def pair(fx, fz, n):
        expand(*((fx, fz, i) for i in GATHER_ORDER[n - 1:n + 1]))

    for n in range(8 + BEHIND):
        if n < 8:
            i = GATHER_ORDER[n]
            arrived = recv_b.at[0, pl.ds(1, 3)] if i == 0 else recv_b.at[i]
            pltpu.make_async_remote_copy(
                arrived, arrived, b_send, b_recv.at[i], device_id=partner_x, device_id_type=MESH
            ).wait_recv()
            z_copy(i).start()
            x_copy(i).start()
            if n % 2:
                pair(0, 0, n)
        m = n - BEHIND
        if m >= 0:
            z_copy(GATHER_ORDER[m]).wait_recv()
            x_copy(8 + GATHER_ORDER[m]).start()
            if m % 2:
                pair(0, 1, m)
    for n in range(1, 8, 2):
        for i in GATHER_ORDER[n - 1:n + 1]:
            x_copy(i).wait_recv()
        pair(1, 0, n)
    for n in range(1, 8, 2):
        for i in GATHER_ORDER[n - 1:n + 1]:
            x_copy(8 + i).wait_recv()
        pair(1, 1, n)

    for sent, sem in (
        (first, first_send), (second, second_send), (send_a.at[pl.ds(1, 31)], a_send),
        (send_b.at[pl.ds(1, 31)], b_send), (recv_z, z_send), (recv_x, x_send),
    ):
        pltpu.make_async_remote_copy(
            sent, sent, sem, a_recv.at[0], device_id=partner_x, device_id_type=MESH
        ).wait_send()
    pltpu.make_async_copy(staged, staged, out_sem).wait()


def per_device(coeff, phase_x, phase_y, phase_q, interp):
    field = (2, K, LANES)
    message = (32, LANES)
    dma = pltpu.SemaphoreType.DMA
    result = pl.pallas_call(
        kernel,
        out_shape=jax.ShapeDtypeStruct((2, K, 32, LANES), F32),
        in_specs=[
            pl.BlockSpec(memory_space=pl.ANY),
            pl.BlockSpec(memory_space=pl.ANY),
            pl.BlockSpec(memory_space=pl.ANY),
        ],
        out_specs=pl.BlockSpec(memory_space=pltpu.VMEM),
        scratch_shapes=[
            pltpu.VMEM((4, 2, 8, K), F32),
            pltpu.VMEM((4, 2, 32, K), F32),
            pltpu.VMEM((4, 2, 32, K), F32),
            pltpu.VMEM((8, 2, 2, *field), F32),
            pltpu.VMEM((8, 2, *field), F32),
            pltpu.VMEM((8, *field), F32),
            pltpu.VMEM((32, *message), F32),
            pltpu.VMEM((32, *message), F32),
            pltpu.VMEM((32, *message), F32),
            pltpu.VMEM((8, 4, *message), F32),
            pltpu.VMEM((8, 4, *message), F32),
            pltpu.VMEM((16, 4, *message), F32),
            pltpu.VMEM((4, 4, *field), F32),
            pltpu.VMEM((8, *field), F32),
            pltpu.VMEM((3, 4, LANES, LANES), F32),
            pltpu.VMEM((3, 8, LANES, LANES), F32),
            pltpu.VMEM((3, 32, LANES, LANES), F32),
            pltpu.VMEM((3, 8, K), F32),
            pltpu.VMEM((3, 8, K), F32),
            pltpu.VMEM((3, 32, K), F32),
            pltpu.VMEM((3, 32, K), F32),
            pltpu.VMEM((4, 2, K, LANES), F32),
            pltpu.VMEM((4, K, LANES), F32),
            pltpu.VMEM((4, K, LANES), F32),
            pltpu.VMEM((32, *field), F32),
            pltpu.VMEM((K, 32 * LANES), F32),
            pltpu.VMEM((32, *field), F32),
            pltpu.VMEM((4 * K, 3 * K), BF16),
            pltpu.VMEM((K, 3 * K), BF16),
            dma((3,)), dma((8,)), dma((2,)), dma, dma((8, 2)), dma, dma((8, 2)),
            dma, dma((2,)), dma, dma((8,)), dma, dma((8,)), dma, dma((16,)), dma,
        ],
        compiler_params=pltpu.CompilerParams(
            collective_id=0, has_side_effects=True, vmem_limit_bytes=51 * 1024 * 1024
        ),
    )(
        coeff.reshape(2, K, 32, LANES),
        jnp.concatenate(
            [phase_x.transpose(0, 1, 3, 2), phase_y.transpose(0, 1, 3, 2), interp.reshape(4, 2, 32, K)], 2
        ),
        phase_q,
    )
    return result.reshape(2, K, 1, 1, 32 * LANES)


def solution(mesh):
    placed = (P(None, None, "gx", "gy", None), P(), P(), P(), P())
    return jax.shard_map(
        per_device,
        mesh=mesh,
        in_specs=placed,
        out_specs=P(None, None, "gx", "gy", None),
        check_vma=False,
    )
```
